32 devices in a mesh: row: 8 (over y, x, core), col: 4 (over z).
Axes of the slice: x: 2, y: 2, z: 4, core: 2. Of those that a mesh axis runs over, the one named last changes fastest.
Arguments:
- high_vectors: float32 [16384, 4096], P('row', 'col'), may hold values from -0.046875 to 0.046875
- high_values: float32 [4096], P('col'), may hold values from 2 to 4
- pool_vectors: float32 [16384, 512], P('row', 'col'), may hold values from -6 to 6
- pool_images: float32 [16384, 512], P('row', 'col'), may hold values from -6 to 6
- pool_values: float32 [512], replicated, may hold values from -2 to 0
- cluster: int32 [256], replicated, may hold values from 0 to 511, as said below
- gap_scale: int32 [256], replicated, may hold values from 1 to 2
Outputs:
- corrected: float32 [16384, 256], P('row', 'col')
The draws below stay inside these ranges and needn't reach their ends.
Inputs may be any that keep to these rules, and one draw needn't show every extreme that they name: Distinct candidate indices; the first and the last candidate are always in the cluster.
All inputs are finite; a program needn't handle non-finite values.
Results may differ from the reference program's by a relative error of at most 0.000084.
Values sent between devices are 32-bit elements; how exact they have to be, the bound alone decides.
No kernel may reach another device: no remote copies, remote signals or barrier semaphores. Data moves between devices by JAX's collectives and lax.ppermute only.
A program may use at most 64 MiB of HBM per device.

```python
import jax
import jax.numpy as jnp
from jax import lax

ROW_DEV = 2048
LOW = 256
POOL = 512
ROWS = 16384
K = 4096
N_ROW = 8


def draw_cluster(key, part):
    inner = jax.random.permutation(jax.random.fold_in(key, 11), POOL - 2)[:LOW - 2] + 1
    ends = jnp.array([0, POOL - 1], jnp.int32)
    joined = jnp.concatenate([inner.astype(jnp.int32), ends])
    return jax.random.permutation(jax.random.fold_in(key, 17), joined).astype(jnp.int32)


def set_ends(drawn, rng, least, largest):
    longest = drawn.shape.index(max(drawn.shape))
    spots = []
    for shift in (0, 1):
        where = [jax.random.randint(jax.random.fold_in(rng, axis), (), 0, length) for axis, length in enumerate(drawn.shape)]
        where[longest] = (where[longest] + shift) % drawn.shape[longest]
        spots.append(tuple(where))
    return drawn.at[spots[0]].set(least).at[spots[1]].set(largest)


def steps_of(own_key, dims, pieces, smallest, largest):
    def one(dim, parts):
        heights = jax.random.uniform(jax.random.fold_in(jax.random.fold_in(own_key, 6), dim), (parts,), jnp.float32, smallest / len(pieces), largest / len(pieces))
        return jnp.repeat(jnp.exp(heights), dims[dim] // parts).reshape((-1,) + (1,) * (len(dims) - dim - 1))

    level = one(*pieces[0])
    for cut in pieces[1:]:
        level = level * one(*cut)
    return level


def gaussian(key, shape, spread, reach, split=(), dtype=jnp.bfloat16):
    values = jax.random.normal(key, shape, jnp.float32) * spread
    if len(split) > 0:
        values = steps_of(key, shape, split, -0.22, 0.18) * values
    return jnp.clip(values, min=-reach, max=reach).astype(dtype)


def setup_inputs(seed: int = 0) -> dict:
    key_of = jax.random.split(jax.random.key(seed), 8)
    return {
        "high_vectors": gaussian(key_of[0], (ROWS, K), (ROW_DEV * N_ROW) ** -0.5, 0.046875, ((0, 8), (1, 4)), jnp.float32),
        "high_values": jnp.clip(2.0 + 2.0 * jax.random.uniform(key_of[1], (K,), jnp.float32) ** steps_of(key_of[1], (K,), ((0, 4),), -0.2, 0.2), 2.0, 4.0),
        "pool_vectors": gaussian(key_of[2], (ROWS, POOL), 1.0, 6.0, ((0, 8), (1, 4)), jnp.float32),
        "pool_images": gaussian(key_of[3], (ROWS, POOL), 1.0, 6.0, ((0, 8), (1, 4)), jnp.float32),
        "pool_values": jnp.clip(jax.random.uniform(key_of[4], (POOL,), jnp.float32, -2.0, 0.0), -2.0, 0.0),
        "cluster": draw_cluster(jax.random.fold_in(key_of[7], 71), 0),
        "gap_scale": set_ends(jax.random.randint(key_of[6], (LOW,), 1, 3), jax.random.fold_in(key_of[6], 1), 1, 2).astype(jnp.int32),
    }


def reference(high_vectors, high_values, pool_vectors, pool_images, pool_values, cluster, gap_scale):
    low_vecs = jnp.take(pool_vectors, cluster, axis=1)
    low_imgs = jnp.take(pool_images, cluster, axis=1)
    low_vals = jnp.take(pool_values, cluster, axis=0)
    both = jnp.concatenate([low_vecs, low_imgs], axis=1)
    sums = lax.dot_general(high_vectors, both, (((0,), (0,)), ((), ())), precision=lax.Precision.HIGHEST, preferred_element_type=jnp.float32)
    correlation = sums[:, :LOW]
    mixed = sums[:, LOW:]
    denom = gap_scale.astype(jnp.float32)[None, :] * (high_values[:, None] - low_vals[None, :])
    coeffs = (mixed - low_vals[None, :] * correlation) / denom
    image = jnp.dot(high_vectors, coeffs, precision=lax.Precision.HIGHEST, preferred_element_type=jnp.float32)
    return low_vecs - image
```

```python
import jax
import jax.numpy as jnp
from jax import lax
from jax.sharding import PartitionSpec as P

HIGH = lax.Precision.HIGH
EXACT = lax.Precision.HIGHEST


def dot(a, b, dims, precision):
    return lax.dot_general(
        a, b, (dims, ((), ())), precision=precision, preferred_element_type=jnp.float32
    )


def gather_line(own, axis):
    n = lax.axis_size(axis)
    me = lax.axis_index(axis)
    buffers = [(own, me)]
    from_left = from_right = own
    for step in range(1, n):
        right = [(i, i + 1) for i in range(step - 1, n - 1)]
        left = [(i, i - 1) for i in range(1, n - step + 1)]
        if from_left is from_right and step > 1 and 2 * step > n + 1:
            both = lax.ppermute(from_left, axis, right + left)
        else:
            came_left = lax.ppermute(from_left, axis, right)
            came_right = lax.ppermute(from_right, axis, left)
            if 2 * step < n:
                buffers += [(came_left, me - step), (came_right, me + step)]
                from_left, from_right = came_left, came_right
                continue
            both = came_left + came_right
        buffers.append((both, jnp.where(me >= step, me - step, me + step)))
        from_left = from_right = both
    return [(rows, jnp.where(src < n, src, -1)) for rows, src in buffers]


def scatter_line(blocks, axis):
    n = lax.axis_size(axis)
    me = lax.axis_index(axis)

    def block(k):
        return lax.dynamic_index_in_dim(blocks, jnp.clip(k, 0, n - 1), 0, keepdims=False)

    from_left = from_right = None
    for step in range(1, n):
        hop = n - step
        right, left = block(me + hop), block(me - hop)
        if from_left is not None:
            right, left = right + from_left, left + from_right
        from_left = lax.ppermute(right, axis, [(i, i + 1) for i in range(step)])
        from_right = lax.ppermute(left, axis, [(i, i - 1) for i in range(n - step, n)])
    return block(me) + from_left + from_right


def sum_pairs(x, axis):
    n = lax.axis_size(axis)
    me = lax.axis_index(axis)
    half = x.shape[0] // 2
    mine = (me % 2) * half
    pairs = [(i, i ^ 1) for i in range(n)]
    keep = lax.dynamic_slice_in_dim(x, mine, half, 0)
    give = lax.dynamic_slice_in_dim(x, half - mine, half, 0)
    part = keep + lax.ppermute(give, axis, pairs)
    bits = [1 << b for b in range(1, n.bit_length() - 1)]
    cut = -(-half // (8 * len(bits))) * 8
    pieces = [part[i * cut : min(half, (i + 1) * cut)] for i in range(len(bits))]
    for turn in range(len(bits)):
        for i in range(len(bits)):
            bit = bits[(i + turn) % len(bits)]
            pieces[i] = pieces[i] + lax.ppermute(
                pieces[i], axis, [(d, d ^ bit) for d in range(n)]
            )
    part = jnp.concatenate(pieces, 0)
    other = lax.ppermute(part, axis, pairs)
    first = me % 2 == 0
    return jnp.concatenate(
        [jnp.where(first, part, other), jnp.where(first, other, part)], 0
    )


def correct(room, high_vectors, high_values, pool_vectors, residual, low_vals, cluster, gap, rank):
    n = lax.axis_size("col")
    me = lax.axis_index("col")
    count = cluster.shape[0]
    width = pool_vectors.shape[1]
    source = cluster // width
    spot = cluster % width
    slot = jnp.arange(room, dtype=jnp.int32)
    pick = jnp.logical_and(slot[:, None] == rank[None, :], source[None, :] == me)
    index = jnp.sum(jnp.where(pick, spot[None, :] + 1, 0), axis=1) - 1
    take = (index[:, None] == jnp.arange(width)[None, :]).astype(jnp.float32)
    own = dot(take, residual, ((1,), (1,)), EXACT)

    buffers = gather_line(own, "col")
    products = [dot(rows, high_vectors, ((1,), (0,)), HIGH) for rows, _ in buffers]
    place = jnp.concatenate(
        [
            jnp.logical_and(source[:, None] == src, rank[:, None] == slot[None, :])
            for _, src in buffers
        ],
        axis=1,
    ).astype(jnp.float32)
    sums = dot(place, jnp.concatenate(products, 0), ((1,), (0,)), EXACT)
    sums = sum_pairs(sums, "row")
    coeffs = sums / (gap.astype(jnp.float32)[:, None] * (high_values[None, :] - low_vals[:, None]))
    image = dot(coeffs, high_vectors, ((1,), (1,)), HIGH)
    mine = jnp.logical_and(source[:, None] == me, spot[:, None] == jnp.arange(width)[None, :])
    vecs = dot(mine.astype(jnp.float32), pool_vectors, ((1,), (1,)), EXACT)
    partial = vecs - image
    out = scatter_line(partial.reshape(n, count // n, -1), "col")
    return out.T


def body(high_vectors, high_values, pool_vectors, pool_images, pool_values, cluster, gap_scale):
    width = pool_vectors.shape[1]
    me = lax.axis_index("col")
    values = lax.dynamic_slice_in_dim(pool_values, me * width, width, 0)
    residual = pool_images - values[None, :] * pool_vectors
    low_vals = jnp.take(pool_values, cluster, axis=0)
    source = cluster // width
    order = jnp.arange(cluster.shape[0])
    before = jnp.logical_and(source[:, None] == source[None, :], order[None, :] < order[:, None])
    rank = jnp.sum(before.astype(jnp.int32), axis=1)
    share = cluster.shape[0] // lax.axis_size("col")
    room = min(width, -(-(share + share // 8) // 8) * 8)
    args = (high_vectors, high_values, pool_vectors, residual, low_vals, cluster, gap_scale, rank)
    if room == width:
        return correct(width, *args)
    return lax.cond(
        jnp.max(rank) < room,
        lambda *a: correct(room, *a),
        lambda *a: correct(width, *a),
        *args,
    )


def solution(mesh):
    placed = (P("row", "col"), P("col"), P("row", "col"), P("row", "col"), P(), P(), P())
    return jax.shard_map(
        body, mesh=mesh, in_specs=placed, out_specs=P("row", "col"), check_vma=False
    )
```

```python
import functools

import jax
import jax.numpy as jnp
from jax import lax
from jax.experimental import pallas as pl
from jax.experimental.pallas import tpu as pltpu
from jax.sharding import PartitionSpec as P

HIGH = lax.Precision.HIGH
EXACT = lax.Precision.HIGHEST
BF16 = jnp.bfloat16
F32 = jnp.float32


def dot(a, b, dims, precision=None):
    return lax.dot_general(
        a, b, (dims, ((), ())), precision=precision, preferred_element_type=F32
    )


PARTS = 2
VMEM = pl.BlockSpec(memory_space=pltpu.VMEM)
SMEM = pl.BlockSpec(memory_space=pltpu.SMEM)


def split(x, count):
    pieces = []
    for _ in range(count):
        piece = x.astype(BF16)
        x = x - piece.astype(F32)
        pieces.append(piece)
    return pieces


def total(terms):
    return functools.reduce(lambda a, b: a + b, terms)


def steps(x, size, count):
    return total([jnp.where(x >= float(k * size), 1.0, 0.0) for k in range(1, count)])


def plan_kernel(n, parts, room, me_ref, cluster_ref, gap_ref, values_ref, vectors_ref, images_ref, info_ref, own_ref):
    count = cluster_ref.shape[1]
    width = vectors_ref.shape[1]
    pool = values_ref.shape[1]
    share = count // n
    square = (count, count)

    def lanes(row):
        return jnp.broadcast_to(row, square)

    me = me_ref[0]
    across = lax.broadcasted_iota(jnp.int32, square, 1).astype(F32)
    down = lax.broadcasted_iota(jnp.int32, square, 0).astype(F32)
    column = lanes(cluster_ref[...].astype(F32))
    source = steps(column, width, n)
    target = steps(across, share, n)
    source_t, target_t = source.T, target.T
    ahead = jnp.logical_or(
        source_t < source, jnp.logical_and(source_t == source, down < across)
    )
    turn = jnp.sum(
        jnp.where(jnp.logical_and(target_t == target, ahead), 1.0, 0.0), axis=0, keepdims=True
    )
    inner = steps(turn, parts, share // parts)
    row = (turn - parts * inner) * (count // parts) + target[:1] * (share // parts) + inner
    row = lanes(row)
    chosen = down == row

    def pick(values):
        return jnp.sum(jnp.where(chosen, lanes(values.astype(F32)), 0.0), axis=1, keepdims=True)

    spot = pick(cluster_ref[...])
    gap = pick(gap_ref[...])
    every = lax.broadcasted_iota(jnp.int32, (count, pool), 1).astype(F32)
    value = jnp.sum(jnp.where(every == spot, values_ref[...], 0.0), axis=1, keepdims=True)
    spots = lanes(spot)
    spots_t = spots.T
    part = steps(down, count // parts, parts)
    part_t = steps(across, count // parts, parts)
    source = steps(spots, width, n)
    source_t = steps(spots_t, width, n)
    peers = jnp.logical_and(jnp.logical_and(source == source_t, part == part_t), spots_t < spots)
    rank = jnp.sum(jnp.where(peers, 1.0, 0.0), axis=1, keepdims=True)
    wide = info_ref.shape[1]
    lane = lax.broadcasted_iota(jnp.int32, (count, wide), 1)
    info = jnp.zeros((count, wide), F32)
    for k, col in enumerate((spot, rank, value, gap, row.T[:, :1])):
        info = jnp.where(lane == k, col, info)
    info_ref[...] = info

    base = (me * width).astype(F32)
    here = lax.broadcasted_iota(jnp.int32, (count, width), 1).astype(F32) + base == spot
    slots = -(-parts * room // 128) * 128
    slot = lax.broadcasted_iota(jnp.int32, (count, slots), 1).astype(F32)
    filled = jnp.logical_and(slot == part[:, :1] * room + rank, rank < float(room))
    take = dot(
        jnp.where(filled, 1.0, 0.0).T[: parts * room].astype(BF16),
        jnp.where(here, 1.0, 0.0).astype(BF16),
        ((1,), (0,)),
    ).astype(BF16)
    lane = lax.broadcasted_iota(jnp.int32, (pool, width), 0)
    wanted = lane == lax.broadcasted_iota(jnp.int32, (pool, width), 1) + me * width
    values = jnp.sum(jnp.where(wanted, values_ref[...].T, 0.0), axis=0, keepdims=True)
    residual = images_ref[...] - values * vectors_ref[...]
    packed = total([dot(take, piece, ((1,), (1,))) for piece in split(residual, 3)])
    for p in range(parts):
        own_ref[p] = packed[p * room : (p + 1) * room]


def plan(room, me, cluster, gap, pool_values, pool_vectors, pool_images):
    rows = pool_vectors.shape[0]
    count = cluster.shape[0]
    n = lax.axis_size("col")
    return pl.pallas_call(
        functools.partial(plan_kernel, n, PARTS, room),
        out_shape=(
            jax.ShapeDtypeStruct((count, 128), F32),
            jax.ShapeDtypeStruct((PARTS, room, rows), F32),
        ),
        in_specs=[SMEM] + [VMEM] * 5,
        out_specs=(VMEM, VMEM),
        compiler_params=pltpu.CompilerParams(vmem_limit_bytes=24 << 20),
    )(me[None], cluster[None, :], gap[None, :], pool_values[None, :], pool_vectors, pool_images)


def product_kernel(width, n, source_ref, info_ref, *refs):
    *buffers, high_ref, out_ref = refs
    room = buffers[0].shape[0]
    slots = room * len(buffers)
    rows = info_ref.shape[0]
    lane = lax.broadcasted_iota(jnp.int32, (rows, slots), 1)
    owner = jnp.full((rows, slots), -1, jnp.int32)
    for b in range(len(buffers)):
        inside = jnp.logical_and(lane >= b * room, lane < (b + 1) * room)
        owner = jnp.where(inside, source_ref[b], owner)
    slot = lax.broadcasted_iota(jnp.int32, (rows, slots), 1).astype(F32)
    slot = slot - room * steps(slot, room, len(buffers))
    place = jnp.logical_and(
        steps(info_ref[:, 0:1], width, n) == owner.astype(F32), info_ref[:, 1:2] == slot
    )
    place = jnp.where(place, 1.0, 0.0).astype(BF16)
    gathered = jnp.concatenate([b[...] for b in buffers], 0)
    high, low = (dot(place, p, ((1,), (0,))).astype(BF16) for p in split(gathered, 2))
    x_high, x_low = split(high_ref[...], 2)
    term = dot(high, x_high, ((1,), (0,))) + dot(low, x_high, ((1,), (0,)))
    term = term + dot(high, x_low, ((1,), (0,)))

    @pl.when(pl.program_id(0) == 0)
    def _():
        out_ref[...] = term

    @pl.when(pl.program_id(0) > 0)
    def _():
        out_ref[...] += term


def product(part, width, info, buffers, high_vectors):
    n = lax.axis_size("col")
    rows, k = high_vectors.shape
    count = info.shape[0] // PARTS
    room = buffers[0][0].shape[0]
    piece = min(rows, 256)
    sources = jnp.stack([jnp.asarray(src, jnp.int32) for _, src in buffers])
    return pl.pallas_call(
        functools.partial(product_kernel, width, n),
        out_shape=jax.ShapeDtypeStruct((count, k), F32),
        grid=(rows // piece,),
        in_specs=[SMEM, pl.BlockSpec((count, info.shape[1]), lambda i: (part, 0))]
        + [pl.BlockSpec((room, piece), lambda i: (0, i)) for _ in buffers]
        + [pl.BlockSpec((piece, k), lambda i: (i, 0))],
        out_specs=pl.BlockSpec((count, k), lambda i: (0, 0)),
        compiler_params=pltpu.CompilerParams(vmem_limit_bytes=24 << 20),
        cost_estimate=pl.CostEstimate(
            flops=6 * count * rows * k, bytes_accessed=4 * rows * k, transcendentals=0
        ),
    )(sources, info, *[b for b, _ in buffers], high_vectors)


def image_kernel(me_ref, info_ref, sums_ref, mu_ref, vectors_ref, high_ref, out_ref, d_high, d_low):
    @pl.when(pl.program_id(0) == 0)
    def _():
        gaps = info_ref[:, 3:4] * (mu_ref[...] - info_ref[:, 2:3])
        high, low = split(sums_ref[...] / gaps, 2)
        d_high[...] = high
        d_low[...] = low

    width = vectors_ref.shape[1]
    spot = lax.broadcasted_iota(jnp.int32, (info_ref.shape[0], width), 1) + me_ref[0] * width
    mine = jnp.where(spot.astype(F32) == info_ref[:, 0:1], 1.0, 0.0).astype(BF16)
    chosen = total([dot(mine, p, ((1,), (1,))) for p in split(vectors_ref[...], 3)])
    x_high, x_low = split(high_ref[...], 2)
    image = dot(d_high[...], x_high, ((1,), (1,))) + dot(d_low[...], x_high, ((1,), (1,)))
    out_ref[...] = chosen - (image + dot(d_high[...], x_low, ((1,), (1,))))


def image(part, me, info, sums, high_values, pool_vectors, high_vectors):
    rows, k = high_vectors.shape
    count = sums.shape[0]
    piece = min(rows, 256)
    return pl.pallas_call(
        image_kernel,
        out_shape=jax.ShapeDtypeStruct((count, rows), F32),
        grid=(rows // piece,),
        in_specs=[
            SMEM,
            pl.BlockSpec((count, info.shape[1]), lambda i: (part, 0)),
            pl.BlockSpec((count, k), lambda i: (0, 0)),
            pl.BlockSpec((1, k), lambda i: (0, 0)),
            pl.BlockSpec((piece, pool_vectors.shape[1]), lambda i: (i, 0)),
            pl.BlockSpec((piece, k), lambda i: (i, 0)),
        ],
        out_specs=pl.BlockSpec((count, piece), lambda i: (0, i)),
        scratch_shapes=[pltpu.VMEM((count, k), BF16)] * 2,
        compiler_params=pltpu.CompilerParams(vmem_limit_bytes=24 << 20),
        cost_estimate=pl.CostEstimate(
            flops=6 * count * rows * k, bytes_accessed=4 * rows * k, transcendentals=0
        ),
    )(me[None], info, sums, high_values[None, :], pool_vectors, high_vectors)


def finish_kernel(parts, me_ref, info_ref, *refs):
    *terms, out_ref = refs
    share = out_ref.shape[0]
    inner = share // parts
    each = len(terms) // parts
    rows = [total([t[...] for t in terms[p * each : (p + 1) * each]]) for p in range(parts)]
    rows = jnp.concatenate(rows, 0)
    first = me_ref[0] * share
    where = info_ref[pl.ds(pl.multiple_of(first, share), share), :][:, 4:5]
    slot = lax.broadcasted_iota(jnp.int32, (share, share), 1).astype(F32)
    part = steps(slot, inner, parts)
    count = info_ref.shape[0]
    row = part * (count // parts) + (me_ref[0] * inner).astype(F32) + (slot - part * inner)
    order = jnp.where(row == where, 1.0, 0.0).astype(BF16)
    out_ref[...] = total([dot(order, p, ((1,), (0,))) for p in split(rows, 3)])


def finish(me, info, terms):
    n = lax.axis_size("col")
    rows = terms[0].shape[1]
    return pl.pallas_call(
        functools.partial(finish_kernel, PARTS),
        out_shape=jax.ShapeDtypeStruct((info.shape[0] // n, rows), F32),
        in_specs=[SMEM] + [VMEM] * (len(terms) + 1),
        out_specs=VMEM,
        compiler_params=pltpu.CompilerParams(vmem_limit_bytes=24 << 20),
    )(me[None], info, *terms)


def mirrored(n, pairs):
    return pairs + [(n - 1 - a, n - 1 - b) for a, b in pairs]


def gather_line(own, axis):
    n = lax.axis_size(axis)
    me = lax.axis_index(axis)
    buffers = [(own, me)]
    from_left = from_right = own
    for step in range(1, n):
        right = [(i, i + 1) for i in range(step - 1, n - 1)]
        left = [(i, i - 1) for i in range(1, n - step + 1)]
        if 2 * step > n + 1:
            rows = lax.ppermute(from_left, axis, right + left)
        else:
            came_left = lax.ppermute(from_left, axis, right)
            came_right = lax.ppermute(from_right, axis, left)
            if 2 * step < n:
                buffers += [(came_left, me - step), (came_right, me + step)]
                from_left, from_right = came_left, came_right
                continue
            rows = came_left + came_right
        buffers.append((rows, jnp.where(me >= step, me - step, me + step)))
        from_left = from_right = rows
    return [(rows, jnp.where(src < n, src, -1)) for rows, src in buffers]


def scatter_line(blocks, axis):
    n = lax.axis_size(axis)
    me = lax.axis_index(axis)
    half = n // 2
    place = me % half
    base = me - place
    left = me < half

    def block(k):
        return lax.dynamic_index_in_dim(blocks, k, 0, keepdims=False)

    terms = [block(me)]
    for target in range(n - 1, half - 1, -1):
        part = block(jnp.where(left, target, n - 1 - target))
        rows = part
        for hop in range(half - 1):
            rows = part + lax.ppermute(rows, axis, mirrored(n, [(hop, hop + 1)]))
        terms.append(lax.ppermute(rows, axis, mirrored(n, [(half - 1, target)])))
    for step in range(1, half):
        turn = [(g + i, g + (i + step) % half) for g in (0, half) for i in range(half)]
        terms.append(lax.ppermute(block(base + (place + step) % half), axis, turn))
    return terms


def sum_pairs(x, axis):
    n = lax.axis_size(axis)
    me = lax.axis_index(axis)
    half = x.shape[0] // 2
    mine = (me % 2) * half
    pairs = [(i, i ^ 1) for i in range(n)]
    keep = lax.dynamic_slice_in_dim(x, mine, half, 0)
    give = lax.dynamic_slice_in_dim(x, half - mine, half, 0)
    part = keep + lax.ppermute(give, axis, pairs)
    bits = [1 << b for b in range(1, n.bit_length() - 1)]
    cut = -(-half // (8 * len(bits))) * 8
    pieces = [part[i * cut : min(half, (i + 1) * cut)] for i in range(len(bits))]
    for turn in range(len(bits)):
        for i in range(len(bits)):
            bit = bits[(i + turn) % len(bits)]
            pieces[i] = pieces[i] + lax.ppermute(
                pieces[i], axis, [(d, d ^ bit) for d in range(n)]
            )
        pieces = list(lax.optimization_barrier(tuple(pieces)))
    part = jnp.concatenate(pieces, 0)
    other = lax.ppermute(part, axis, pairs)
    first = me % 2 == 0
    return jnp.concatenate(
        [jnp.where(first, part, other), jnp.where(first, other, part)], 0
    )


def correct_parts(room, high_vectors, high_values, pool_vectors, pool_images, pool_values, cluster, gap):
    n = lax.axis_size("col")
    me = lax.axis_index("col")
    count = cluster.shape[0]
    width = pool_vectors.shape[1]
    info, own = plan(room, me, cluster, gap, pool_values, pool_vectors, pool_images)
    gathered = [gather_line(own[p], "col") for p in range(PARTS)]
    sums = [
        sum_pairs(product(p, width, info, gathered[p], high_vectors), "row") for p in range(PARTS)
    ]
    terms = []
    for p in range(PARTS):
        partial = image(p, me, info, sums[p], high_values, pool_vectors, high_vectors)
        terms += scatter_line(partial.reshape(n, count // (n * PARTS), -1), "col")
    return finish(me, info, terms).T, jnp.max(info[:, 1]) + 1.0


def correct_whole(high_vectors, high_values, pool_vectors, pool_images, pool_values, cluster, gap):
    n = lax.axis_size("col")
    me = lax.axis_index("col")
    count = cluster.shape[0]
    width = pool_vectors.shape[1]
    low_vals = jnp.take(pool_values, cluster, axis=0)
    values = lax.dynamic_slice_in_dim(pool_values, me * width, width, 0)
    own = (pool_images - values[None, :] * pool_vectors).T
    sums = jnp.zeros((count, high_vectors.shape[1]), F32)
    for rows, source in gather_line(own, "col"):
        spot = source * width + jnp.arange(width)
        here = jnp.logical_and(cluster[:, None] == spot[None, :], source >= 0).astype(F32)
        rows = dot(here, rows, ((1,), (0,)), EXACT)
        sums = sums + dot(rows, high_vectors, ((1,), (0,)), HIGH)
    sums = sum_pairs(sums, "row")
    coeffs = sums / (gap.astype(F32)[:, None] * (high_values[None, :] - low_vals[:, None]))
    mine = (cluster[:, None] == me * width + jnp.arange(width)[None, :]).astype(F32)
    partial = dot(mine, pool_vectors, ((1,), (1,)), EXACT)
    partial = partial - dot(coeffs, high_vectors, ((1,), (1,)), HIGH)
    return total(scatter_line(partial.reshape(n, count // n, -1), "col")).T


def body(*args):
    width = args[2].shape[1]
    share = args[5].shape[0] // (PARTS * lax.axis_size("col"))
    room = min(width, -(-(share + share // 4) // 8) * 8)
    out, most = correct_parts(room, *args)
    if room == width:
        return out
    return lax.cond(most <= room, lambda *_: out, correct_whole, *args)


def solution(mesh):
    placed = (P("row", "col"), P("col"), P("row", "col"), P("row", "col"), P(), P(), P())
    return jax.shard_map(
        body, mesh=mesh, in_specs=placed, out_specs=P("row", "col"), check_vma=False
    )
```

```python
import functools

import jax
import jax.numpy as jnp
from jax import lax
from jax.experimental import pallas as pl
from jax.experimental.pallas import tpu as pltpu
from jax.sharding import PartitionSpec as P

HIGH = lax.Precision.HIGH
EXACT = lax.Precision.HIGHEST
BF16 = jnp.bfloat16
F32 = jnp.float32


def dot(a, b, dims, precision=None):
    return lax.dot_general(
        a, b, (dims, ((), ())), precision=precision, preferred_element_type=F32
    )


PARTS = 2
VMEM = pl.BlockSpec(memory_space=pltpu.VMEM)
SMEM = pl.BlockSpec(memory_space=pltpu.SMEM)


def split(x, count):
    pieces = []
    for _ in range(count):
        piece = x.astype(BF16)
        x = x - piece.astype(F32)
        pieces.append(piece)
    return pieces


def total(terms):
    return functools.reduce(lambda a, b: a + b, terms)


def steps(x, size, count):
    return total([jnp.where(x >= float(k * size), 1.0, 0.0) for k in range(1, count)])


def plan_kernel(n, parts, room, me_ref, cluster_ref, gap_ref, values_ref, vectors_ref, images_ref, info_ref, own_ref):
    count = cluster_ref.shape[1]
    width = vectors_ref.shape[1]
    pool = values_ref.shape[1]
    share = count // n
    square = (count, count)

    def lanes(row):
        return jnp.broadcast_to(row, square)

    me = me_ref[0]
    across = lax.broadcasted_iota(jnp.int32, square, 1).astype(F32)
    down = lax.broadcasted_iota(jnp.int32, square, 0).astype(F32)
    column = lanes(cluster_ref[...].astype(F32))
    source = steps(column, width, n)
    target = steps(across, share, n)
    source_t, target_t = source.T, target.T
    ahead = jnp.logical_or(
        source_t < source, jnp.logical_and(source_t == source, down < across)
    )
    turn = jnp.sum(
        jnp.where(jnp.logical_and(target_t == target, ahead), 1.0, 0.0), axis=0, keepdims=True
    )
    inner = steps(turn, parts, share // parts)
    row = (turn - parts * inner) * (count // parts) + target[:1] * (share // parts) + inner
    row = lanes(row)
    chosen = down == row

    def pick(values):
        return jnp.sum(jnp.where(chosen, lanes(values.astype(F32)), 0.0), axis=1, keepdims=True)

    spot = pick(cluster_ref[...])
    gap = pick(gap_ref[...])
    every = lax.broadcasted_iota(jnp.int32, (count, pool), 1).astype(F32)
    value = jnp.sum(jnp.where(every == spot, values_ref[...], 0.0), axis=1, keepdims=True)
    spots = lanes(spot)
    spots_t = spots.T
    part = steps(down, count // parts, parts)
    part_t = steps(across, count // parts, parts)
    source = steps(spots, width, n)
    source_t = steps(spots_t, width, n)
    peers = jnp.logical_and(jnp.logical_and(source == source_t, part == part_t), spots_t < spots)
    rank = jnp.sum(jnp.where(peers, 1.0, 0.0), axis=1, keepdims=True)
    wide = info_ref.shape[2]
    lane = lax.broadcasted_iota(jnp.int32, (count, wide), 1)
    info = jnp.zeros((count, wide), F32)
    for k, col in enumerate((spot, rank, value, gap, row.T[:, :1])):
        info = jnp.where(lane == k, col, info)
    for p in range(parts):
        info_ref[p] = info[p * (count // parts) : (p + 1) * (count // parts)]

    base = (me * width).astype(F32)
    here = lax.broadcasted_iota(jnp.int32, (count, width), 1).astype(F32) + base == spot
    slots = -(-parts * room // 128) * 128
    slot = lax.broadcasted_iota(jnp.int32, (count, slots), 1).astype(F32)
    filled = jnp.logical_and(slot == part[:, :1] * room + rank, rank < float(room))
    take = dot(
        jnp.where(filled, 1.0, 0.0).T[: parts * room].astype(BF16),
        jnp.where(here, 1.0, 0.0).astype(BF16),
        ((1,), (0,)),
    ).astype(BF16)
    lane = lax.broadcasted_iota(jnp.int32, (pool, width), 0)
    wanted = lane == lax.broadcasted_iota(jnp.int32, (pool, width), 1) + me * width
    values = jnp.sum(jnp.where(wanted, values_ref[...].T, 0.0), axis=0, keepdims=True)
    residual = images_ref[...] - values * vectors_ref[...]
    packed = total([dot(take, piece, ((1,), (1,))) for piece in split(residual, 3)])
    for p in range(parts):
        own_ref[p] = packed[p * room : (p + 1) * room]


def plan(room, me, cluster, gap, pool_values, pool_vectors, pool_images):
    rows = pool_vectors.shape[0]
    count = cluster.shape[0]
    n = lax.axis_size("col")
    return pl.pallas_call(
        functools.partial(plan_kernel, n, PARTS, room),
        out_shape=(
            jax.ShapeDtypeStruct((PARTS, count // PARTS, 128), F32),
            jax.ShapeDtypeStruct((PARTS, room, rows), F32),
        ),
        in_specs=[SMEM] + [VMEM] * 5,
        out_specs=(VMEM, VMEM),
        compiler_params=pltpu.CompilerParams(vmem_limit_bytes=24 << 20),
    )(me[None], cluster[None, :], gap[None, :], pool_values[None, :], pool_vectors, pool_images)


def product_kernel(width, n, source_ref, info_ref, *refs):
    *buffers, high_ref, out_ref = refs
    room = buffers[0].shape[0]
    slots = room * len(buffers)
    rows = info_ref.shape[0]
    lane = lax.broadcasted_iota(jnp.int32, (rows, slots), 1)
    owner = jnp.full((rows, slots), -1, jnp.int32)
    for b in range(len(buffers)):
        inside = jnp.logical_and(lane >= b * room, lane < (b + 1) * room)
        owner = jnp.where(inside, source_ref[b], owner)
    slot = lane.astype(F32)
    slot = slot - room * steps(slot, room, len(buffers))
    place = jnp.logical_and(
        steps(info_ref[:, 0:1], width, n) == owner.astype(F32), info_ref[:, 1:2] == slot
    )
    place = jnp.where(place, 1.0, 0.0).astype(BF16)
    depth = high_ref.shape[0]
    piece = min(depth, 512)
    terms = []
    for start in range(0, depth, piece):
        span = slice(start, start + piece)
        gathered = jnp.concatenate([b[:, span] for b in buffers], 0)
        high, low = (dot(place, p, ((1,), (0,))).astype(BF16) for p in split(gathered, 2))
        x_high, x_low = split(high_ref[span], 2)
        left = jnp.concatenate([high, low, high], 1)
        terms.append(dot(left, jnp.concatenate([x_high, x_high, x_low], 0), ((1,), (0,))))
    out_ref[...] = total(terms)


def cost(count, high_vectors):
    rows, k = high_vectors.shape
    return pl.CostEstimate(
        flops=6 * count * rows * k, bytes_accessed=4 * rows * k, transcendentals=0
    )


def product(width, info, buffers, high_vectors):
    n = lax.axis_size("col")
    count = info.shape[0]
    sources = jnp.stack([jnp.asarray(src, jnp.int32) for _, src in buffers])
    return pl.pallas_call(
        functools.partial(product_kernel, width, n),
        out_shape=jax.ShapeDtypeStruct((count, high_vectors.shape[1]), F32),
        in_specs=[SMEM] + [VMEM] * (len(buffers) + 2),
        out_specs=VMEM,
        compiler_params=pltpu.CompilerParams(vmem_limit_bytes=40 << 20),
        cost_estimate=cost(count, high_vectors),
    )(sources, info, *[b for b, _ in buffers], high_vectors)


def image_kernel(me_ref, info_ref, sums_ref, mu_ref, vectors_ref, high_ref, out_ref):
    count = info_ref.shape[0]
    gaps = info_ref[:, 3:4] * (mu_ref[...] - info_ref[:, 2:3])
    d_high, d_low = split(sums_ref[...] / gaps, 2)
    both = jnp.concatenate([d_high, d_low], 0)
    width = vectors_ref.shape[1]
    spot = lax.broadcasted_iota(jnp.int32, (count, width), 1) + me_ref[0] * width
    mine = jnp.where(spot.astype(F32) == info_ref[:, 0:1], 1.0, 0.0).astype(BF16)
    depth = high_ref.shape[0]
    piece = min(depth, 256)
    for start in range(0, depth, piece):
        span = slice(start, start + piece)
        chosen = total([dot(mine, p, ((1,), (1,))) for p in split(vectors_ref[span], 3)])
        x_high, x_low = split(high_ref[span], 2)
        image = dot(both, x_high, ((1,), (1,)))
        image = image[:count] + image[count:] + dot(d_high, x_low, ((1,), (1,)))
        out_ref[:, span] = chosen - image


def image(me, info, sums, high_values, pool_vectors, high_vectors):
    count = info.shape[0]
    return pl.pallas_call(
        image_kernel,
        out_shape=jax.ShapeDtypeStruct((count, high_vectors.shape[0]), F32),
        in_specs=[SMEM] + [VMEM] * 5,
        out_specs=VMEM,
        compiler_params=pltpu.CompilerParams(vmem_limit_bytes=40 << 20),
        cost_estimate=cost(count, high_vectors),
    )(me[None], info, sums, high_values[None, :], pool_vectors, high_vectors)


def finish_kernel(parts, me_ref, info_ref, *refs):
    *terms, out_ref = refs
    share = out_ref.shape[0]
    inner = share // parts
    each = len(terms) // parts
    rows = [total([t[...] for t in terms[p * each : (p + 1) * each]]) for p in range(parts)]
    rows = jnp.concatenate(rows, 0)
    first = me_ref[0] * share
    where = info_ref[pl.ds(pl.multiple_of(first, share), share), :][:, 4:5]
    slot = lax.broadcasted_iota(jnp.int32, (share, share), 1).astype(F32)
    part = steps(slot, inner, parts)
    count = info_ref.shape[0]
    row = part * (count // parts) + (me_ref[0] * inner).astype(F32) + (slot - part * inner)
    order = jnp.where(row == where, 1.0, 0.0).astype(BF16)
    out_ref[...] = total([dot(order, p, ((1,), (0,))) for p in split(rows, 3)])


def finish(me, info, terms):
    n = lax.axis_size("col")
    rows = terms[0].shape[1]
    return pl.pallas_call(
        functools.partial(finish_kernel, PARTS),
        out_shape=jax.ShapeDtypeStruct((info.shape[0] // n, rows), F32),
        in_specs=[SMEM] + [VMEM] * (len(terms) + 1),
        out_specs=VMEM,
        compiler_params=pltpu.CompilerParams(vmem_limit_bytes=24 << 20),
    )(me[None], info, *terms)


def mirrored(n, pairs):
    return pairs + [(n - 1 - a, n - 1 - b) for a, b in pairs]


def gather_line(own, axis):
    n = lax.axis_size(axis)
    me = lax.axis_index(axis)
    buffers = [(own, me)]
    from_left = from_right = own
    for step in range(1, n):
        right = [(i, i + 1) for i in range(step - 1, n - 1)]
        left = [(i, i - 1) for i in range(1, n - step + 1)]
        if 2 * step > n + 1:
            rows = lax.ppermute(from_left, axis, right + left)
        else:
            came_left = lax.ppermute(from_left, axis, right)
            came_right = lax.ppermute(from_right, axis, left)
            if 2 * step < n:
                buffers += [(came_left, me - step), (came_right, me + step)]
                from_left, from_right = came_left, came_right
                continue
            rows = came_left + came_right
        buffers.append((rows, jnp.where(me >= step, me - step, me + step)))
        from_left = from_right = rows
    return [(rows, jnp.where(src < n, src, -1)) for rows, src in buffers]


def scatter_line(blocks, axis):
    n = lax.axis_size(axis)
    me = lax.axis_index(axis)
    half = n // 2
    place = me % half
    base = me - place
    left = me < half

    def block(k):
        return lax.dynamic_index_in_dim(blocks, k, 0, keepdims=False)

    terms = [block(me)]
    for target in range(n - 1, half - 1, -1):
        part = block(jnp.where(left, target, n - 1 - target))
        rows = part
        for hop in range(half - 1):
            rows = part + lax.ppermute(rows, axis, mirrored(n, [(hop, hop + 1)]))
        terms.append(lax.ppermute(rows, axis, mirrored(n, [(half - 1, target)])))
    for step in range(1, half):
        turn = [(g + i, g + (i + step) % half) for g in (0, half) for i in range(half)]
        terms.append(lax.ppermute(block(base + (place + step) % half), axis, turn))
    return terms


def sum_pairs(x, axis):
    n = lax.axis_size(axis)
    me = lax.axis_index(axis)
    half = x.shape[0] // 2
    mine = (me % 2) * half
    pairs = [(i, i ^ 1) for i in range(n)]
    keep = lax.dynamic_slice_in_dim(x, mine, half, 0)
    give = lax.dynamic_slice_in_dim(x, half - mine, half, 0)
    part = keep + lax.ppermute(give, axis, pairs)
    bits = [1 << b for b in range(1, n.bit_length() - 1)]
    cut = -(-half // (8 * len(bits))) * 8
    pieces = [part[i * cut : min(half, (i + 1) * cut)] for i in range(len(bits))]
    for turn in range(len(bits)):
        for i in range(len(bits)):
            bit = bits[(i + turn) % len(bits)]
            pieces[i] = pieces[i] + lax.ppermute(
                pieces[i], axis, [(d, d ^ bit) for d in range(n)]
            )
        pieces = list(lax.optimization_barrier(tuple(pieces)))
    part = jnp.concatenate(pieces, 0)
    other = lax.ppermute(part, axis, pairs)
    first = me % 2 == 0
    return jnp.concatenate(
        [jnp.where(first, part, other), jnp.where(first, other, part)], 0
    )


def correct_parts(room, high_vectors, high_values, pool_vectors, pool_images, pool_values, cluster, gap):
    n = lax.axis_size("col")
    me = lax.axis_index("col")
    count = cluster.shape[0]
    width = pool_vectors.shape[1]
    info, own = plan(room, me, cluster, gap, pool_values, pool_vectors, pool_images)
    gathered = [gather_line(own[p], "col") for p in range(PARTS)]
    sums = [
        sum_pairs(product(width, info[p], gathered[p], high_vectors), "row") for p in range(PARTS)
    ]
    terms = []
    for p in range(PARTS):
        partial = image(me, info[p], sums[p], high_values, pool_vectors, high_vectors)
        terms += scatter_line(partial.reshape(n, count // (n * PARTS), -1), "col")
    return finish(me, info.reshape(count, -1), terms).T, jnp.max(info[:, :, 1]) + 1.0


def correct_whole(high_vectors, high_values, pool_vectors, pool_images, pool_values, cluster, gap):
    n = lax.axis_size("col")
    me = lax.axis_index("col")
    count = cluster.shape[0]
    width = pool_vectors.shape[1]
    low_vals = jnp.take(pool_values, cluster, axis=0)
    values = lax.dynamic_slice_in_dim(pool_values, me * width, width, 0)
    own = (pool_images - values[None, :] * pool_vectors).T
    sums = jnp.zeros((count, high_vectors.shape[1]), F32)
    for rows, source in gather_line(own, "col"):
        spot = source * width + jnp.arange(width)
        here = jnp.logical_and(cluster[:, None] == spot[None, :], source >= 0).astype(F32)
        rows = dot(here, rows, ((1,), (0,)), EXACT)
        sums = sums + dot(rows, high_vectors, ((1,), (0,)), HIGH)
    sums = sum_pairs(sums, "row")
    coeffs = sums / (gap.astype(F32)[:, None] * (high_values[None, :] - low_vals[:, None]))
    mine = (cluster[:, None] == me * width + jnp.arange(width)[None, :]).astype(F32)
    partial = dot(mine, pool_vectors, ((1,), (1,)), EXACT)
    partial = partial - dot(coeffs, high_vectors, ((1,), (1,)), HIGH)
    return total(scatter_line(partial.reshape(n, count // n, -1), "col")).T


def body(*args):
    width = args[2].shape[1]
    share = args[5].shape[0] // (PARTS * lax.axis_size("col"))
    room = min(width, -(-(share + share // 4) // 8) * 8)
    out, most = correct_parts(room, *args)
    if room == width:
        return out
    return lax.cond(most <= room, lambda *_: out, correct_whole, *args)


def solution(mesh):
    placed = (P("row", "col"), P("col"), P("row", "col"), P("row", "col"), P(), P(), P())
    return jax.shard_map(
        body, mesh=mesh, in_specs=placed, out_specs=P("row", "col"), check_vma=False
    )
```

```python
import functools

import jax
import jax.numpy as jnp
from jax import lax
from jax.experimental import pallas as pl
from jax.experimental.pallas import tpu as pltpu
from jax.sharding import PartitionSpec as P

HIGH = lax.Precision.HIGH
EXACT = lax.Precision.HIGHEST
BF16 = jnp.bfloat16
F32 = jnp.float32


def dot(a, b, dims, precision=None):
    return lax.dot_general(
        a, b, (dims, ((), ())), precision=precision, preferred_element_type=F32
    )


PARTS = 2
VMEM = pl.BlockSpec(memory_space=pltpu.VMEM)
SMEM = pl.BlockSpec(memory_space=pltpu.SMEM)


def split(x, count):
    pieces = []
    for _ in range(count):
        piece = x.astype(BF16)
        x = x - piece.astype(F32)
        pieces.append(piece)
    return pieces


def total(terms):
    return functools.reduce(lambda a, b: a + b, terms)


def steps(x, size, count):
    return total([jnp.where(x >= float(k * size), 1.0, 0.0) for k in range(1, count)])


def plan_kernel(n, parts, room, me_ref, cluster_ref, gap_ref, values_ref, vectors_ref, images_ref, info_ref, own_ref):
    count = cluster_ref.shape[1]
    width = vectors_ref.shape[1]
    pool = values_ref.shape[1]
    share = count // n
    square = (count, count)

    def lanes(row):
        return jnp.broadcast_to(row, square)

    me = me_ref[0]
    across = lax.broadcasted_iota(jnp.int32, square, 1).astype(F32)
    down = lax.broadcasted_iota(jnp.int32, square, 0).astype(F32)
    column = lanes(cluster_ref[...].astype(F32))
    source = steps(column, width, n)
    target = steps(across, share, n)
    source_t, target_t = source.T, target.T
    ahead = jnp.logical_or(
        source_t < source, jnp.logical_and(source_t == source, down < across)
    )
    turn = jnp.sum(
        jnp.where(jnp.logical_and(target_t == target, ahead), 1.0, 0.0), axis=0, keepdims=True
    )
    inner = steps(turn, parts, share // parts)
    row = (turn - parts * inner) * (count // parts) + target[:1] * (share // parts) + inner
    row = lanes(row)
    chosen = down == row

    def pick(values):
        return jnp.sum(jnp.where(chosen, lanes(values.astype(F32)), 0.0), axis=1, keepdims=True)

    spot = pick(cluster_ref[...])
    gap = pick(gap_ref[...])
    every = lax.broadcasted_iota(jnp.int32, (count, pool), 1).astype(F32)
    value = jnp.sum(jnp.where(every == spot, values_ref[...], 0.0), axis=1, keepdims=True)
    spots = lanes(spot)
    spots_t = spots.T
    part = steps(down, count // parts, parts)
    part_t = steps(across, count // parts, parts)
    source = steps(spots, width, n)
    source_t = steps(spots_t, width, n)
    peers = jnp.logical_and(jnp.logical_and(source == source_t, part == part_t), spots_t < spots)
    rank = jnp.sum(jnp.where(peers, 1.0, 0.0), axis=1, keepdims=True)
    wide = info_ref.shape[2]
    lane = lax.broadcasted_iota(jnp.int32, (count, wide), 1)
    info = jnp.zeros((count, wide), F32)
    for k, col in enumerate((spot, rank, value, gap, row.T[:, :1])):
        info = jnp.where(lane == k, col, info)
    for p in range(parts):
        info_ref[p] = info[p * (count // parts) : (p + 1) * (count // parts)]

    base = (me * width).astype(F32)
    here = lax.broadcasted_iota(jnp.int32, (count, width), 1).astype(F32) + base == spot
    slots = -(-parts * room // 128) * 128
    slot = lax.broadcasted_iota(jnp.int32, (count, slots), 1).astype(F32)
    filled = jnp.logical_and(slot == part[:, :1] * room + rank, rank < float(room))
    take = dot(
        jnp.where(filled, 1.0, 0.0).T[: parts * room].astype(BF16),
        jnp.where(here, 1.0, 0.0).astype(BF16),
        ((1,), (0,)),
    ).astype(BF16)
    lane = lax.broadcasted_iota(jnp.int32, (pool, width), 0)
    wanted = lane == lax.broadcasted_iota(jnp.int32, (pool, width), 1) + me * width
    values = jnp.sum(jnp.where(wanted, values_ref[...].T, 0.0), axis=0, keepdims=True)
    residual = images_ref[...] - values * vectors_ref[...]
    packed = total([dot(take, piece, ((1,), (1,))) for piece in split(residual, 3)])
    for p in range(parts):
        own_ref[p] = packed[p * room : (p + 1) * room]


def plan(room, me, cluster, gap, pool_values, pool_vectors, pool_images):
    rows = pool_vectors.shape[0]
    count = cluster.shape[0]
    n = lax.axis_size("col")
    return pl.pallas_call(
        functools.partial(plan_kernel, n, PARTS, room),
        out_shape=(
            jax.ShapeDtypeStruct((PARTS, count // PARTS, 128), F32),
            jax.ShapeDtypeStruct((PARTS, room, rows), F32),
        ),
        in_specs=[SMEM] + [VMEM] * 5,
        out_specs=(VMEM, VMEM),
        compiler_params=pltpu.CompilerParams(vmem_limit_bytes=24 << 20),
    )(me[None], cluster[None, :], gap[None, :], pool_values[None, :], pool_vectors, pool_images)


def pieces_of(x_ref, step):
    rows = x_ref.shape[0]
    step = min(rows, step)
    for start in range(0, rows, step):
        span = slice(start, start + step)
        yield span, split(x_ref[span], 2)


def product_kernel(width, n, scalar_ref, info_ref, *refs):
    *buffers, x_ref, keep_ref, give_ref = refs
    room = buffers[0].shape[0]
    slots = room * len(buffers)
    rows = info_ref.shape[0]
    half = rows // 2
    mine = pl.multiple_of(scalar_ref[len(buffers)] * half, half)
    info = jnp.concatenate(
        [info_ref[pl.ds(mine, half), :], info_ref[pl.ds(half - mine, half), :]], 0
    )
    lane = lax.broadcasted_iota(jnp.int32, (rows, slots), 1)
    owner = jnp.full((rows, slots), -1, jnp.int32)
    for b in range(len(buffers)):
        inside = jnp.logical_and(lane >= b * room, lane < (b + 1) * room)
        owner = jnp.where(inside, scalar_ref[b], owner)
    slot = lane.astype(F32)
    slot = slot - room * steps(slot, room, len(buffers))
    place = jnp.logical_and(
        steps(info[:, 0:1], width, n) == owner.astype(F32), info[:, 1:2] == slot
    )
    place = jnp.where(place, 1.0, 0.0).astype(BF16)
    terms = []
    for span, (x_high, x_low) in pieces_of(x_ref, 512):
        gathered = jnp.concatenate([b[:, span] for b in buffers], 0)
        high, low = (dot(place, p, ((1,), (0,))).astype(BF16) for p in split(gathered, 2))
        left = jnp.concatenate([high, low, high], 1)
        terms.append(dot(left, jnp.concatenate([x_high, x_high, x_low], 0), ((1,), (0,))))
    out = total(terms)
    keep_ref[...] = out[:half]
    give_ref[...] = out[half:]


def cost(count, high_vectors):
    rows, k = high_vectors.shape
    return pl.CostEstimate(
        flops=6 * count * rows * k, bytes_accessed=4 * rows * k, transcendentals=0
    )


def product(width, pair, info, buffers, high_vectors):
    n = lax.axis_size("col")
    count = info.shape[0]
    scalars = jnp.stack([jnp.asarray(src, jnp.int32) for _, src in buffers] + [pair])
    return pl.pallas_call(
        functools.partial(product_kernel, width, n),
        out_shape=[jax.ShapeDtypeStruct((count // 2, high_vectors.shape[1]), F32)] * 2,
        in_specs=[SMEM] + [VMEM] * (len(buffers) + 2),
        out_specs=[VMEM, VMEM],
        compiler_params=pltpu.CompilerParams(vmem_limit_bytes=24 << 20),
        cost_estimate=cost(count, high_vectors),
    )(scalars, info, *[b for b, _ in buffers], high_vectors)


def image_kernel(pieces, scalar_ref, info_ref, mu_ref, vectors_ref, x_ref, *refs):
    sums, outs = refs[: 2 * pieces], refs[2 * pieces :]
    *outs, sums_ref = outs
    count = info_ref.shape[0]
    block = outs[0].shape[0]
    first = scalar_ref[len(outs) + 1] == 0
    mine = jnp.concatenate([r[...] for r in sums[:pieces]], 0)
    pair = jnp.concatenate([r[...] for r in sums[pieces:]], 0)
    sums_ref[: count // 2] = jnp.where(first, mine, pair)
    sums_ref[count // 2 :] = jnp.where(first, pair, mine)

    def ordered(ref):
        spans = [
            pl.ds(pl.multiple_of(scalar_ref[k] * block, block), block) for k in range(len(outs))
        ]
        return jnp.concatenate([ref[span, :] for span in spans], 0)

    info = ordered(info_ref)
    gaps = info[:, 3:4] * (mu_ref[...] - info[:, 2:3])
    d_high, d_low = split(ordered(sums_ref) / gaps, 2)
    both = jnp.concatenate([d_high, d_low], 0)
    width = vectors_ref.shape[1]
    spot = lax.broadcasted_iota(jnp.int32, (count, width), 1) + scalar_ref[len(outs)] * width
    mine = jnp.where(spot.astype(F32) == info[:, 0:1], 1.0, 0.0).astype(BF16)
    for span, (x_high, x_low) in pieces_of(x_ref, 256):
        chosen = total([dot(mine, p, ((1,), (1,))) for p in split(vectors_ref[span], 3)])
        image = dot(both, x_high, ((1,), (1,)))
        image = image[:count] + image[count:] + dot(d_high, x_low, ((1,), (1,)))
        for k, out in enumerate(outs):
            rows = slice(k * block, (k + 1) * block)
            out[:, span] = chosen[rows] - image[rows]


def image(order, me, pair, info, sums, high_values, pool_vectors, high_vectors):
    count = info.shape[0]
    block = count // len(order)
    depth, k = high_vectors.shape
    scalars = jnp.stack([jnp.asarray(i, jnp.int32) for i in [*order, me, pair]])
    return pl.pallas_call(
        functools.partial(image_kernel, len(sums) // 2),
        out_shape=[jax.ShapeDtypeStruct((block, depth), F32)] * len(order),
        in_specs=[SMEM] + [VMEM] * (len(sums) + 4),
        out_specs=[VMEM] * len(order),
        scratch_shapes=[pltpu.VMEM((count, k), F32)],
        compiler_params=pltpu.CompilerParams(vmem_limit_bytes=24 << 20),
        cost_estimate=cost(count, high_vectors),
    )(scalars, info, high_values[None, :], pool_vectors, high_vectors, *sums)


def finish_kernel(parts, me_ref, info_ref, *refs):
    *terms, out_ref = refs
    share = out_ref.shape[0]
    inner = share // parts
    each = len(terms) // parts
    rows = [total([t[...] for t in terms[p * each : (p + 1) * each]]) for p in range(parts)]
    rows = jnp.concatenate(rows, 0)
    first = me_ref[0] * share
    where = info_ref[pl.ds(pl.multiple_of(first, share), share), :][:, 4:5]
    slot = lax.broadcasted_iota(jnp.int32, (share, share), 1).astype(F32)
    part = steps(slot, inner, parts)
    count = info_ref.shape[0]
    row = part * (count // parts) + (me_ref[0] * inner).astype(F32) + (slot - part * inner)
    order = jnp.where(row == where, 1.0, 0.0).astype(BF16)
    out_ref[...] = total([dot(order, p, ((1,), (0,))) for p in split(rows, 3)])


def finish(me, info, terms):
    n = lax.axis_size("col")
    rows = terms[0].shape[1]
    return pl.pallas_call(
        functools.partial(finish_kernel, PARTS),
        out_shape=jax.ShapeDtypeStruct((info.shape[0] // n, rows), F32),
        in_specs=[SMEM] + [VMEM] * (len(terms) + 1),
        out_specs=VMEM,
        compiler_params=pltpu.CompilerParams(vmem_limit_bytes=24 << 20),
    )(me[None], info, *terms)


def mirrored(n, pairs):
    return pairs + [(n - 1 - a, n - 1 - b) for a, b in pairs]


def gather_line(own, axis):
    n = lax.axis_size(axis)
    me = lax.axis_index(axis)
    buffers = [(own, me)]
    from_left = from_right = own
    for step in range(1, n):
        right = [(i, i + 1) for i in range(step - 1, n - 1)]
        left = [(i, i - 1) for i in range(1, n - step + 1)]
        if 2 * step > n + 1:
            rows = lax.ppermute(from_left, axis, right + left)
        else:
            came_left = lax.ppermute(from_left, axis, right)
            came_right = lax.ppermute(from_right, axis, left)
            if 2 * step < n:
                buffers += [(came_left, me - step), (came_right, me + step)]
                from_left, from_right = came_left, came_right
                continue
            rows = came_left + came_right
        buffers.append((rows, jnp.where(me >= step, me - step, me + step)))
        from_left = from_right = rows
    return [(rows, jnp.where(src < n, src, -1)) for rows, src in buffers]


def scatter_order(axis):
    n = lax.axis_size(axis)
    me = lax.axis_index(axis)
    half = n // 2
    place = me % half
    near = [me - place + (place + step) % half for step in range(half)]
    return near + [jnp.where(me < half, k, n - 1 - k) for k in range(n - 1, half - 1, -1)]


def scatter_line(blocks, axis):
    n = lax.axis_size(axis)
    half = n // 2
    terms = [blocks[0]]
    for target in range(n - 1, half - 1, -1):
        part = rows = blocks[half + n - 1 - target]
        for hop in range(half - 1):
            came = lax.ppermute(rows, axis, mirrored(n, [(hop, hop + 1)]))
            rows = part + came
        terms.append(lax.ppermute(rows, axis, mirrored(n, [(half - 1, target)])))
    for step in range(1, half):
        turn = [(g + i, g + (i + step) % half) for g in (0, half) for i in range(half)]
        terms.append(lax.ppermute(blocks[step], axis, turn))
    return terms


def sum_pairs(keep, give, axis):
    n = lax.axis_size(axis)
    pairs = [(i, i ^ 1) for i in range(n)]
    half = keep.shape[0]
    part = keep + lax.ppermute(give, axis, pairs)
    bits = [1 << b for b in range(1, n.bit_length() - 1)]
    cut = -(-half // (8 * len(bits))) * 8
    pieces = [part[i * cut : min(half, (i + 1) * cut)] for i in range(len(bits))]
    for turn in range(len(bits)):
        for i in range(len(bits)):
            bit = bits[(i + turn) % len(bits)]
            pieces[i] = pieces[i] + lax.ppermute(
                pieces[i], axis, [(d, d ^ bit) for d in range(n)]
            )
        pieces = list(lax.optimization_barrier(tuple(pieces)))
    return pieces, [lax.ppermute(p, axis, pairs) for p in pieces]


def correct_parts(room, high_vectors, high_values, pool_vectors, pool_images, pool_values, cluster, gap):
    me = lax.axis_index("col")
    pair = lax.axis_index("row") % 2
    count = cluster.shape[0]
    width = pool_vectors.shape[1]
    info, own = plan(room, me, cluster, gap, pool_values, pool_vectors, pool_images)
    order = scatter_order("col")
    terms = []
    for p in range(PARTS):
        gathered = gather_line(own[p], "col")
        keep, give = product(width, pair, info[p], gathered, high_vectors)
        mine, other = sum_pairs(keep, give, "row")
        blocks = image(order, me, pair, info[p], mine + other, high_values, pool_vectors, high_vectors)
        terms += scatter_line(blocks, "col")
    return finish(me, info.reshape(count, -1), terms).T, jnp.max(info[:, :, 1]) + 1.0


def correct_whole(high_vectors, high_values, pool_vectors, pool_images, pool_values, cluster, gap):
    n = lax.axis_size("col")
    me = lax.axis_index("col")
    pair = lax.axis_index("row") % 2
    count = cluster.shape[0]
    width = pool_vectors.shape[1]
    low_vals = jnp.take(pool_values, cluster, axis=0)
    values = lax.dynamic_slice_in_dim(pool_values, me * width, width, 0)
    own = (pool_images - values[None, :] * pool_vectors).T
    sums = jnp.zeros((count, high_vectors.shape[1]), F32)
    for rows, source in gather_line(own, "col"):
        spot = source * width + jnp.arange(width)
        here = jnp.logical_and(cluster[:, None] == spot[None, :], source >= 0).astype(F32)
        rows = dot(here, rows, ((1,), (0,)), EXACT)
        sums = sums + dot(rows, high_vectors, ((1,), (0,)), HIGH)
    half = count // 2
    keep = lax.dynamic_slice_in_dim(sums, pair * half, half, 0)
    give = lax.dynamic_slice_in_dim(sums, half - pair * half, half, 0)
    mine, other = (jnp.concatenate(p, 0) for p in sum_pairs(keep, give, "row"))
    first = pair == 0
    sums = jnp.concatenate([jnp.where(first, mine, other), jnp.where(first, other, mine)], 0)
    coeffs = sums / (gap.astype(F32)[:, None] * (high_values[None, :] - low_vals[:, None]))
    mine = (cluster[:, None] == me * width + jnp.arange(width)[None, :]).astype(F32)
    partial = dot(mine, pool_vectors, ((1,), (1,)), EXACT)
    partial = partial - dot(coeffs, high_vectors, ((1,), (1,)), HIGH)
    blocks = partial.reshape(n, count // n, -1)
    blocks = [lax.dynamic_index_in_dim(blocks, k, 0, keepdims=False) for k in scatter_order("col")]
    return total(scatter_line(blocks, "col")).T


def body(*args):
    width = args[2].shape[1]
    share = args[5].shape[0] // (PARTS * lax.axis_size("col"))
    room = min(width, -(-(share + share // 4) // 8) * 8)
    out, most = correct_parts(room, *args)
    if room == width:
        return out
    return lax.cond(most <= room, lambda *_: out, correct_whole, *args)


def solution(mesh):
    placed = (P("row", "col"), P("col"), P("row", "col"), P("row", "col"), P(), P(), P())
    return jax.shard_map(
        body, mesh=mesh, in_specs=placed, out_specs=P("row", "col"), check_vma=False
    )
```

```python
import functools

import jax
import jax.numpy as jnp
from jax import lax
from jax.experimental import pallas as pl
from jax.experimental.pallas import tpu as pltpu
from jax.sharding import PartitionSpec as P

HIGH = lax.Precision.HIGH
EXACT = lax.Precision.HIGHEST
BF16 = jnp.bfloat16
F32 = jnp.float32


def dot(a, b, dims, precision=None):
    return lax.dot_general(
        a, b, (dims, ((), ())), precision=precision, preferred_element_type=F32
    )


PARTS = 2
VMEM = pl.BlockSpec(memory_space=pltpu.VMEM)
SMEM = pl.BlockSpec(memory_space=pltpu.SMEM)
HBM = pl.BlockSpec(memory_space=pltpu.HBM)


def split(x, count):
    pieces = []
    for _ in range(count):
        piece = x.astype(BF16)
        x = x - piece.astype(F32)
        pieces.append(piece)
    return pieces


def total(terms):
    return functools.reduce(lambda a, b: a + b, terms)


def steps(x, size, count):
    return total([jnp.where(x >= float(k * size), 1.0, 0.0) for k in range(1, count)])


def plan_kernel(n, parts, room, me_ref, cluster_ref, gap_ref, values_ref, vectors_ref, images_ref, info_ref, own_ref):
    count = cluster_ref.shape[1]
    width = vectors_ref.shape[1]
    pool = values_ref.shape[1]
    share = count // n
    square = (count, count)

    def lanes(row):
        return jnp.broadcast_to(row, square)

    me = me_ref[0]
    across = lax.broadcasted_iota(jnp.int32, square, 1).astype(F32)
    down = lax.broadcasted_iota(jnp.int32, square, 0).astype(F32)
    column = lanes(cluster_ref[...].astype(F32))
    source = steps(column, width, n)
    target = steps(across, share, n)
    source_t, target_t = source.T, target.T
    ahead = jnp.logical_or(
        source_t < source, jnp.logical_and(source_t == source, down < across)
    )
    turn = jnp.sum(
        jnp.where(jnp.logical_and(target_t == target, ahead), 1.0, 0.0), axis=0, keepdims=True
    )
    inner = steps(turn, parts, share // parts)
    row = (turn - parts * inner) * (count // parts) + target[:1] * (share // parts) + inner
    row = lanes(row)
    chosen = down == row

    def pick(values):
        return jnp.sum(jnp.where(chosen, lanes(values.astype(F32)), 0.0), axis=1, keepdims=True)

    spot = pick(cluster_ref[...])
    gap = pick(gap_ref[...])
    every = lax.broadcasted_iota(jnp.int32, (count, pool), 1).astype(F32)
    value = jnp.sum(jnp.where(every == spot, values_ref[...], 0.0), axis=1, keepdims=True)
    spots = lanes(spot)
    spots_t = spots.T
    part = steps(down, count // parts, parts)
    part_t = steps(across, count // parts, parts)
    source = steps(spots, width, n)
    source_t = steps(spots_t, width, n)
    peers = jnp.logical_and(jnp.logical_and(source == source_t, part == part_t), spots_t < spots)
    rank = jnp.sum(jnp.where(peers, 1.0, 0.0), axis=1, keepdims=True)
    wide = info_ref.shape[2]
    lane = lax.broadcasted_iota(jnp.int32, (count, wide), 1)
    info = jnp.zeros((count, wide), F32)
    for k, col in enumerate((spot, rank, value, gap, row.T[:, :1])):
        info = jnp.where(lane == k, col, info)
    for p in range(parts):
        info_ref[p] = info[p * (count // parts) : (p + 1) * (count // parts)]

    base = (me * width).astype(F32)
    here = lax.broadcasted_iota(jnp.int32, (count, width), 1).astype(F32) + base == spot
    slots = -(-parts * room // 128) * 128
    slot = lax.broadcasted_iota(jnp.int32, (count, slots), 1).astype(F32)
    filled = jnp.logical_and(slot == part[:, :1] * room + rank, rank < float(room))
    take = dot(
        jnp.where(filled, 1.0, 0.0).T[: parts * room].astype(BF16),
        jnp.where(here, 1.0, 0.0).astype(BF16),
        ((1,), (0,)),
    ).astype(BF16)
    lane = lax.broadcasted_iota(jnp.int32, (pool, width), 0)
    wanted = lane == lax.broadcasted_iota(jnp.int32, (pool, width), 1) + me * width
    values = jnp.sum(jnp.where(wanted, values_ref[...].T, 0.0), axis=0, keepdims=True)
    residual = images_ref[...] - values * vectors_ref[...]
    packed = total([dot(take, piece, ((1,), (1,))) for piece in split(residual, 3)])
    for p in range(parts):
        own_ref[p] = packed[p * room : (p + 1) * room]


def plan(room, me, cluster, gap, pool_values, pool_vectors, pool_images):
    rows = pool_vectors.shape[0]
    count = cluster.shape[0]
    n = lax.axis_size("col")
    return pl.pallas_call(
        functools.partial(plan_kernel, n, PARTS, room),
        out_shape=(
            jax.ShapeDtypeStruct((PARTS, count // PARTS, 128), F32),
            jax.ShapeDtypeStruct((PARTS, room, rows), F32),
        ),
        in_specs=[SMEM] + [VMEM] * 5,
        out_specs=(VMEM, VMEM),
        compiler_params=pltpu.CompilerParams(vmem_limit_bytes=24 << 20),
    )(me[None], cluster[None, :], gap[None, :], pool_values[None, :], pool_vectors, pool_images)


def pieces_of(x_ref, step):
    rows = x_ref.shape[0]
    step = min(rows, step)
    for start in range(0, rows, step):
        span = slice(start, start + step)
        yield span, split(x_ref[span], 2)


def product_kernel(width, n, scalar_ref, info_ref, *refs):
    *buffers, x_ref, keep_ref, give_ref = refs
    room = buffers[0].shape[0]
    slots = room * len(buffers)
    rows = info_ref.shape[0]
    half = rows // 2
    mine = pl.multiple_of(scalar_ref[len(buffers)] * half, half)
    info = jnp.concatenate(
        [info_ref[pl.ds(mine, half), :], info_ref[pl.ds(half - mine, half), :]], 0
    )
    lane = lax.broadcasted_iota(jnp.int32, (rows, slots), 1)
    owner = jnp.full((rows, slots), -1, jnp.int32)
    for b in range(len(buffers)):
        inside = jnp.logical_and(lane >= b * room, lane < (b + 1) * room)
        owner = jnp.where(inside, scalar_ref[b], owner)
    slot = lane.astype(F32)
    slot = slot - room * steps(slot, room, len(buffers))
    place = jnp.logical_and(
        steps(info[:, 0:1], width, n) == owner.astype(F32), info[:, 1:2] == slot
    )
    place = jnp.where(place, 1.0, 0.0).astype(BF16)
    terms = []
    for span, (x_high, x_low) in pieces_of(x_ref, 512):
        gathered = jnp.concatenate([b[:, span] for b in buffers], 0)
        high, low = (dot(place, p, ((1,), (0,))).astype(BF16) for p in split(gathered, 2))
        left = jnp.concatenate([high, low, high], 1)
        terms.append(dot(left, jnp.concatenate([x_high, x_high, x_low], 0), ((1,), (0,))))
    out = total(terms)
    keep_ref[...] = out[:half]
    give_ref[...] = out[half:]


def cost(count, high_vectors):
    rows, k = high_vectors.shape
    return pl.CostEstimate(
        flops=6 * count * rows * k, bytes_accessed=4 * rows * k, transcendentals=0
    )


def product(width, pair, info, buffers, high_vectors):
    n = lax.axis_size("col")
    count = info.shape[0]
    scalars = jnp.stack([jnp.asarray(src, jnp.int32) for _, src in buffers] + [pair])
    return pl.pallas_call(
        functools.partial(product_kernel, width, n),
        out_shape=[jax.ShapeDtypeStruct((count // 2, high_vectors.shape[1]), F32)] * 2,
        in_specs=[SMEM] + [VMEM] * (len(buffers) + 2),
        out_specs=[VMEM, VMEM],
        compiler_params=pltpu.CompilerParams(vmem_limit_bytes=24 << 20),
        cost_estimate=cost(count, high_vectors),
    )(scalars, info, *[b for b, _ in buffers], high_vectors)


def copies_of(x_ref, held_ref, sems):
    rows = x_ref.shape[0] // sems.shape[0]
    spans = [slice(i * rows, (i + 1) * rows) for i in range(sems.shape[0])]
    copies = [
        pltpu.make_async_copy(
            x_ref.at[pl.ds(i * rows, rows)], held_ref.at[pl.ds(i * rows, rows)], sems.at[i]
        )
        for i in range(len(spans))
    ]
    return list(zip(copies, spans))


def image_kernel(pieces, scalar_ref, info_ref, mu_ref, vectors_ref, x_ref, *refs):
    sums, outs = refs[: 2 * pieces], refs[2 * pieces :]
    *outs, sums_ref, held_ref, sems = outs
    copies = copies_of(x_ref, held_ref, sems)
    for copy, _ in copies:
        copy.start()
    count = info_ref.shape[0]
    block = outs[0].shape[0]
    first = scalar_ref[len(outs) + 1] == 0
    mine = jnp.concatenate([r[...] for r in sums[:pieces]], 0)
    pair = jnp.concatenate([r[...] for r in sums[pieces:]], 0)
    sums_ref[: count // 2] = jnp.where(first, mine, pair)
    sums_ref[count // 2 :] = jnp.where(first, pair, mine)

    def ordered(ref):
        spans = [
            pl.ds(pl.multiple_of(scalar_ref[k] * block, block), block) for k in range(len(outs))
        ]
        return jnp.concatenate([ref[span, :] for span in spans], 0)

    info = ordered(info_ref)
    gaps = info[:, 3:4] * (mu_ref[...] - info[:, 2:3])
    d_high, d_low = split(ordered(sums_ref) / gaps, 2)
    both = jnp.concatenate([d_high, d_low], 0)
    width = vectors_ref.shape[1]
    spot = lax.broadcasted_iota(jnp.int32, (count, width), 1) + scalar_ref[len(outs)] * width
    mine = jnp.where(spot.astype(F32) == info[:, 0:1], 1.0, 0.0).astype(BF16)
    for copy, span in copies:
        copy.wait()
        x_high, x_low = split(held_ref[span], 2)
        chosen = total([dot(mine, p, ((1,), (1,))) for p in split(vectors_ref[span], 3)])
        image = dot(both, x_high, ((1,), (1,)))
        image = image[:count] + image[count:] + dot(d_high, x_low, ((1,), (1,)))
        for k, out in enumerate(outs):
            rows = slice(k * block, (k + 1) * block)
            out[:, span] = chosen[rows] - image[rows]


def image(order, me, pair, info, sums, high_values, pool_vectors, high_vectors):
    count = info.shape[0]
    block = count // len(order)
    depth, k = high_vectors.shape
    scalars = jnp.stack([jnp.asarray(i, jnp.int32) for i in [*order, me, pair]])
    return pl.pallas_call(
        functools.partial(image_kernel, len(sums) // 2),
        out_shape=[jax.ShapeDtypeStruct((block, depth), F32)] * len(order),
        in_specs=[SMEM] + [VMEM] * 3 + [HBM] + [VMEM] * len(sums),
        out_specs=[VMEM] * len(order),
        scratch_shapes=[
            pltpu.VMEM((count, k), F32),
            pltpu.VMEM((depth, k), F32),
            pltpu.SemaphoreType.DMA((4,)),
        ],
        compiler_params=pltpu.CompilerParams(vmem_limit_bytes=24 << 20),
        cost_estimate=cost(count, high_vectors),
    )(scalars, info, high_values[None, :], pool_vectors, high_vectors, *sums)


def finish_kernel(parts, me_ref, info_ref, *refs):
    *terms, out_ref = refs
    share = out_ref.shape[0]
    inner = share // parts
    each = len(terms) // parts
    rows = [total([t[...] for t in terms[p * each : (p + 1) * each]]) for p in range(parts)]
    rows = jnp.concatenate(rows, 0)
    first = me_ref[0] * share
    where = info_ref[pl.ds(pl.multiple_of(first, share), share), :][:, 4:5]
    slot = lax.broadcasted_iota(jnp.int32, (share, share), 1).astype(F32)
    part = steps(slot, inner, parts)
    count = info_ref.shape[0]
    row = part * (count // parts) + (me_ref[0] * inner).astype(F32) + (slot - part * inner)
    order = jnp.where(row == where, 1.0, 0.0).astype(BF16)
    out_ref[...] = total([dot(order, p, ((1,), (0,))) for p in split(rows, 3)])


def finish(me, info, terms):
    n = lax.axis_size("col")
    rows = terms[0].shape[1]
    return pl.pallas_call(
        functools.partial(finish_kernel, PARTS),
        out_shape=jax.ShapeDtypeStruct((info.shape[0] // n, rows), F32),
        in_specs=[SMEM] + [VMEM] * (len(terms) + 1),
        out_specs=VMEM,
        compiler_params=pltpu.CompilerParams(vmem_limit_bytes=24 << 20),
    )(me[None], info, *terms)


def mirrored(n, pairs):
    return pairs + [(n - 1 - a, n - 1 - b) for a, b in pairs]


def gather_line(own, axis):
    n = lax.axis_size(axis)
    me = lax.axis_index(axis)
    buffers = [(own, me)]
    from_left = from_right = own
    for step in range(1, n):
        right = [(i, i + 1) for i in range(step - 1, n - 1)]
        left = [(i, i - 1) for i in range(1, n - step + 1)]
        if 2 * step > n + 1:
            rows = lax.ppermute(from_left, axis, right + left)
        else:
            came_left = lax.ppermute(from_left, axis, right)
            came_right = lax.ppermute(from_right, axis, left)
            if 2 * step < n:
                buffers += [(came_left, me - step), (came_right, me + step)]
                from_left, from_right = came_left, came_right
                continue
            rows = came_left + came_right
        buffers.append((rows, jnp.where(me >= step, me - step, me + step)))
        from_left = from_right = rows
    return [(rows, jnp.where(src < n, src, -1)) for rows, src in buffers]


def scatter_order(axis):
    n = lax.axis_size(axis)
    me = lax.axis_index(axis)
    half = n // 2
    place = me % half
    near = [me - place + (place + step) % half for step in range(half)]
    return near + [jnp.where(me < half, k, n - 1 - k) for k in range(n - 1, half - 1, -1)]


def scatter_line(blocks, axis):
    n = lax.axis_size(axis)
    half = n // 2
    terms = [blocks[0]]
    for target in range(n - 1, half - 1, -1):
        part = rows = blocks[half + n - 1 - target]
        for hop in range(half - 1):
            came = lax.ppermute(rows, axis, mirrored(n, [(hop, hop + 1)]))
            rows = part + came
        terms.append(lax.ppermute(rows, axis, mirrored(n, [(half - 1, target)])))
    for step in range(1, half):
        turn = [(g + i, g + (i + step) % half) for g in (0, half) for i in range(half)]
        terms.append(lax.ppermute(blocks[step], axis, turn))
    return terms


def sum_pairs(keep, give, axis):
    n = lax.axis_size(axis)
    pairs = [(i, i ^ 1) for i in range(n)]
    half = keep.shape[0]
    part = keep + lax.ppermute(give, axis, pairs)
    bits = [1 << b for b in range(1, n.bit_length() - 1)]
    cut = -(-half // (8 * len(bits))) * 8
    pieces = [part[i * cut : min(half, (i + 1) * cut)] for i in range(len(bits))]
    for turn in range(len(bits)):
        for i in range(len(bits)):
            bit = bits[(i + turn) % len(bits)]
            pieces[i] = pieces[i] + lax.ppermute(
                pieces[i], axis, [(d, d ^ bit) for d in range(n)]
            )
        pieces = list(lax.optimization_barrier(tuple(pieces)))
    return pieces, [lax.ppermute(p, axis, pairs) for p in pieces]


def correct_parts(room, high_vectors, high_values, pool_vectors, pool_images, pool_values, cluster, gap):
    me = lax.axis_index("col")
    pair = lax.axis_index("row") % 2
    count = cluster.shape[0]
    width = pool_vectors.shape[1]
    info, own = plan(room, me, cluster, gap, pool_values, pool_vectors, pool_images)
    order = scatter_order("col")
    terms = []
    for p in range(PARTS):
        gathered = gather_line(own[p], "col")
        keep, give = product(width, pair, info[p], gathered, high_vectors)
        mine, other = sum_pairs(keep, give, "row")
        blocks = image(order, me, pair, info[p], mine + other, high_values, pool_vectors, high_vectors)
        terms += scatter_line(blocks, "col")
    return finish(me, info.reshape(count, -1), terms).T, jnp.max(info[:, :, 1]) + 1.0


def correct_whole(high_vectors, high_values, pool_vectors, pool_images, pool_values, cluster, gap):
    n = lax.axis_size("col")
    me = lax.axis_index("col")
    pair = lax.axis_index("row") % 2
    count = cluster.shape[0]
    width = pool_vectors.shape[1]
    low_vals = jnp.take(pool_values, cluster, axis=0)
    values = lax.dynamic_slice_in_dim(pool_values, me * width, width, 0)
    own = (pool_images - values[None, :] * pool_vectors).T
    sums = jnp.zeros((count, high_vectors.shape[1]), F32)
    for rows, source in gather_line(own, "col"):
        spot = source * width + jnp.arange(width)
        here = jnp.logical_and(cluster[:, None] == spot[None, :], source >= 0).astype(F32)
        rows = dot(here, rows, ((1,), (0,)), EXACT)
        sums = sums + dot(rows, high_vectors, ((1,), (0,)), HIGH)
    half = count // 2
    keep = lax.dynamic_slice_in_dim(sums, pair * half, half, 0)
    give = lax.dynamic_slice_in_dim(sums, half - pair * half, half, 0)
    mine, other = (jnp.concatenate(p, 0) for p in sum_pairs(keep, give, "row"))
    first = pair == 0
    sums = jnp.concatenate([jnp.where(first, mine, other), jnp.where(first, other, mine)], 0)
    coeffs = sums / (gap.astype(F32)[:, None] * (high_values[None, :] - low_vals[:, None]))
    mine = (cluster[:, None] == me * width + jnp.arange(width)[None, :]).astype(F32)
    partial = dot(mine, pool_vectors, ((1,), (1,)), EXACT)
    partial = partial - dot(coeffs, high_vectors, ((1,), (1,)), HIGH)
    blocks = partial.reshape(n, count // n, -1)
    blocks = [lax.dynamic_index_in_dim(blocks, k, 0, keepdims=False) for k in scatter_order("col")]
    return total(scatter_line(blocks, "col")).T


def body(*args):
    width = args[2].shape[1]
    share = args[5].shape[0] // (PARTS * lax.axis_size("col"))
    room = min(width, -(-(share + share // 4) // 8) * 8)
    out, most = correct_parts(room, *args)
    if room == width:
        return out
    return lax.cond(most <= room, lambda *_: out, correct_whole, *args)


def solution(mesh):
    placed = (P("row", "col"), P("col"), P("row", "col"), P("row", "col"), P(), P(), P())
    return jax.shard_map(
        body, mesh=mesh, in_specs=placed, out_specs=P("row", "col"), check_vma=False
    )
```
